32 devices in a mesh: dp: 4 (over x, core), seq: 8 (over z, y).
Axes of the slice: x: 2, y: 2, z: 4, core: 2. Of those that a mesh axis runs over, the one named last changes fastest.
Arguments:
- activations: bfloat16 [4, 1024, 768], P('dp', 'seq'), may hold values from -600 to 600
- conv_weight: bfloat16 [3840, 768], replicated, may hold values from -0.09375 to 0.09375
- head_first: bfloat16 [768, 768], replicated, may hold values from -0.21875 to 0.21875
- head_second: bfloat16 [768], replicated, may hold values from -5 to 5
- hidden_cotangent: bfloat16 [4, 1024, 768], P('dp', 'seq'), may hold values from -3 to 3
- score_cotangent: float32 [4, 1024], P('dp', 'seq'), may hold values from -5 to 5
- donor_row: int32 [4, 1024], P('dp', 'seq'), may hold values from 0 to 127
- acceptor_owner: int32 [4, 1024, 1], P('dp', 'seq'), may hold values from 0 to 7; in each aligned block of 128 rows (0 to 127, 128 to 255, ..., all dimensions but the last counted through in order) at most 32 rows name the same one
- acceptor_row: int32 [4, 1024], P('dp', 'seq'), may hold values from 0 to 127
Outputs:
- input_grad: bfloat16 [4, 1024, 768], P('dp', 'seq')
- weight_grads: float32 [4608, 768], P('seq', 'dp')
The draws below stay inside these ranges and needn't reach their ends.
Inputs may be any that keep to these rules, and one draw needn't show every extreme that they name: `acceptor_owner`: among the 128 pairs of one block of positions, no block index is named by more than 32 pairs, a bound that some block reaches in every draw.
All inputs are finite; a program needn't handle non-finite values.
Results may differ from the reference program's by a relative error of at most 0.01.
Values may be sent and summed in bfloat16 or wider, within the bound.
A program may use at most 64 MiB of HBM per device.

```python
import math
import jax
import jax.numpy as jnp
import numpy as np
from jax import lax

CHANNELS = 768
OUT_CHANNELS = 768
TAPS = 5
DILATION = 8
ROWS_DEV = 128
PAIRS_DEV = 128
BATCH = 4
SEQ_LEN = 1024
PAIRS = 1024
CAPACITY = 32
N_SEQ = 8


def draw_activations(key, part):
    key_base, key_rows, key_columns = jax.random.split(key, 3)
    shape_full = (BATCH, SEQ_LEN, CHANNELS)
    values = jnp.clip(jax.random.normal(key_base, shape_full, jnp.float32), -6.0, 6.0)
    row_scale = jnp.exp(jax.random.uniform(key_rows, (BATCH, SEQ_LEN, 1), jnp.float32, 0.0, math.log(10.0)))
    column_scale = jnp.exp(jax.random.uniform(key_columns, (1, 1, CHANNELS), jnp.float32, 0.0, math.log(10.0)))
    return (values * row_scale * column_scale).astype(jnp.bfloat16)


def place_ends(values, key, smallest, high):
    extent = values.shape
    place = [jax.random.randint(jax.random.fold_in(key, axis), (), 0, extent[axis]) for axis in range(len(extent))]
    values = values.at[tuple(place)].set(smallest)
    longest = extent.index(max(extent))
    place[longest] = (place[longest] + 1) % extent[longest]
    return values.at[tuple(place)].set(high)


def level_of(stream_key, shape, pieces, low, high):
    level, own = 1.0, jax.random.fold_in(stream_key, 6)
    for position, blocks in pieces:
        draws = jnp.exp(jax.random.uniform(jax.random.fold_in(own, position), (blocks,), jnp.float32, low / len(pieces), high / len(pieces)))
        level = level * jnp.repeat(draws, shape[position] // blocks).reshape([-1 if axis == position else 1 for axis in range(len(shape))])
    return level


def shared_out(own_key, own, number, rows, amount, top, reach, slope):
    ranking = jax.random.permutation(own_key, amount)
    crowded, usual = portions_of(amount, rows * top, reach, slope, True), portions_of(amount, rows * top, reach, slope, False)
    places = jnp.arange(amount)

    def named(tallies, offset_by):
        used = int((tallies > 0).sum())
        fixed = max(1, used // 4)
        shifted = fixed + (places - fixed + offset_by * (used - fixed)) % max(1, amount - fixed)
        return jnp.zeros((amount,), jnp.int32).at[ranking[jnp.where(places < fixed, places, shifted)]].set(jnp.asarray(tallies, jnp.int32))

    tallies = jnp.where(number % 4 == 0, named(crowded, number // 4), named(usual, number - number // 4 - 1))
    mixed = jax.random.permutation(jax.random.fold_in(own, 3), amount)
    source_of, taker = mixed[0:amount // 2 * 2:2], mixed[1:amount // 2 * 2:2]
    margin = jnp.minimum(tallies[source_of] - 1, reach - tallies[taker]) // 2
    margin = jnp.where((source_of == ranking[0]) | (taker == ranking[0]) | (tallies[taker] == 0), 0, jnp.maximum(margin, 0))
    shifted = jax.random.randint(jax.random.fold_in(own, 4), (amount // 2,), 0, 1 << 20) % (margin + 1)
    tallies = tallies.at[source_of].add(-shifted).at[taker].add(shifted)
    items = jnp.searchsorted(jnp.cumsum(tallies), jnp.arange(rows * top), side="right").astype(jnp.int32)
    table = items.reshape(top, rows).T
    table = table[jax.random.permutation(jax.random.fold_in(own, 1), rows)]
    offset_by = jax.random.randint(jax.random.fold_in(own, 2), (rows, 1), 0, top)
    return jnp.take_along_axis(table, (jnp.arange(top)[None, :] + offset_by) % top, axis=1)


def portions_of(count, total, most, lean, full):
    portions = [(1 << 20) // math.isqrt(rank ** lean) + 1 for rank in range(1, count + 1)]
    largest = most if full else min(most, max(-(-total // count), total * portions[0] // sum(portions)))
    least = 1 if total - largest >= count - 1 else 0
    holding, surplus = [largest] + [least] * (count - 1), total - largest - least * (count - 1)
    while surplus > 0:
        movable = [i for i in range(1, count) if holding[i] < largest] or [i for i in range(1, count) if holding[i] < most]
        mass, left = sum([portions[i] for i in movable]), surplus
        for i in movable:
            more = min(most - holding[i], max(1, left * portions[i] // mass), surplus)
            holding[i] = holding[i] + more
            surplus = surplus - more
    return np.array(holding)


def gaussian(rng, extent, spread, bound, shards=(), kind=jnp.bfloat16):
    entries = spread * jax.random.normal(rng, extent, jnp.float32)
    if shards:
        entries = entries * level_of(rng, extent, shards, -0.22, 0.18)
    return jnp.clip(entries, -bound, bound).astype(kind)


def setup_inputs(seed: int = 0) -> dict:
    splits = jax.random.split(jax.random.key(seed), 10)
    activations = draw_activations(jax.random.fold_in(splits[9], 71), 0)
    conv_weight = gaussian(splits[1], (TAPS * CHANNELS, OUT_CHANNELS), (TAPS * CHANNELS) ** -0.5, 0.09375)
    head_first = gaussian(splits[2], (OUT_CHANNELS, OUT_CHANNELS), OUT_CHANNELS ** -0.5, 0.21875)
    head_second = gaussian(splits[3], (OUT_CHANNELS,), 1.0, 5.0)
    hidden_cotangent = gaussian(splits[4], (BATCH, SEQ_LEN, OUT_CHANNELS), 0.5, 3.0, ((0, 4), (1, 8)))
    score_cotangent = gaussian(splits[5], (BATCH, PAIRS), 1.0, 5.0, ((0, 4), (1, 8)), jnp.float32)
    donor_row = place_ends(jax.random.randint(splits[6], (BATCH, PAIRS), 0, ROWS_DEV), jax.random.fold_in(splits[6], 1), 0, ROWS_DEV - 1).astype(jnp.int32)
    acceptor_owner_keys = jax.random.split(jax.random.fold_in(splits[7], 1), BATCH * PAIRS // PAIRS_DEV)
    acceptor_owner_turns = jax.random.permutation(jax.random.fold_in(splits[7], 3), BATCH * PAIRS // PAIRS_DEV)
    acceptor_owner = jax.vmap(lambda own, number: shared_out(jax.random.fold_in(splits[7], 2), own, number, PAIRS_DEV, N_SEQ, 1, CAPACITY, 2))(acceptor_owner_keys, acceptor_owner_turns).reshape((BATCH, PAIRS, 1))
    acceptor_row = place_ends(jax.random.randint(splits[8], (BATCH, PAIRS), 0, ROWS_DEV), jax.random.fold_in(splits[8], 1), 0, ROWS_DEV - 1).astype(jnp.int32)
    return dict(activations=activations, conv_weight=conv_weight, head_first=head_first, head_second=head_second, hidden_cotangent=hidden_cotangent, score_cotangent=score_cotangent, donor_row=donor_row, acceptor_owner=acceptor_owner, acceptor_row=acceptor_row)


def gelu_slope(values):
    normal_cdf = 0.5 * (1.0 + lax.erf(values * (1.0 / math.sqrt(2.0))))
    density = jnp.exp(-0.5 * values * values) * (1.0 / math.sqrt(2.0 * math.pi))
    return normal_cdf + values * density

def contract_rows(left_side, right_side):
    return lax.dot_general(left_side, right_side, (((0,), (0,)), ((), ())), preferred_element_type=jnp.float32)

def reference(activations, conv_weight, head_first, head_second, hidden_cotangent, score_cotangent, donor_row, acceptor_owner, acceptor_row):
    reach_rows = (TAPS - 1) // 2 * DILATION
    shard_of_pair = jnp.arange(PAIRS, dtype=jnp.int32) // PAIRS_DEV
    conv_total = jnp.zeros((TAPS * CHANNELS, OUT_CHANNELS), jnp.float32)
    head_total = jnp.zeros((OUT_CHANNELS, OUT_CHANNELS), jnp.float32)
    grads_out = []
    for batch_index in range(BATCH):
        input_values = activations[batch_index].astype(jnp.float32)
        norm_inverse = lax.rsqrt(lax.optimization_barrier(jnp.mean(input_values * input_values, axis=1, keepdims=True)) + 1e-05)
        normed = (input_values * norm_inverse).astype(jnp.bfloat16)
        padded = jnp.pad(normed, ((reach_rows, reach_rows), (0, 0)))
        preact = jnp.zeros((SEQ_LEN, OUT_CHANNELS), jnp.float32)
        for tap_index in range(TAPS):
            first_row = tap_index * DILATION
            preact = preact + jnp.dot(padded[first_row:first_row + SEQ_LEN], conv_weight[tap_index * CHANNELS:(tap_index + 1) * CHANNELS], preferred_element_type=jnp.float32)
        hidden = jax.nn.gelu(preact, approximate=False).astype(jnp.bfloat16)
        donor_pos = (shard_of_pair * ROWS_DEV + donor_row[batch_index]).astype(jnp.int32)
        accept_pos = (acceptor_owner[batch_index, :, 0] * ROWS_DEV + acceptor_row[batch_index]).astype(jnp.int32)
        donor_values = hidden[donor_pos].astype(jnp.float32)
        accept_values = hidden[accept_pos].astype(jnp.float32)
        pair_feature = (donor_values * accept_values).astype(jnp.bfloat16)
        head_preact = jnp.dot(pair_feature, head_first, preferred_element_type=jnp.float32)
        head_delta = (score_cotangent[batch_index][:, None] * head_second.astype(jnp.float32)[None, :] * gelu_slope(head_preact)).astype(jnp.bfloat16)
        feature_grad = lax.dot_general(head_delta, head_first, (((1,), (1,)), ((), ())), preferred_element_type=jnp.float32)
        donor_grad = (feature_grad * accept_values).astype(jnp.bfloat16)
        accept_grad = (feature_grad * donor_values).astype(jnp.bfloat16)
        hidden_grad = hidden_cotangent[batch_index].astype(jnp.float32)
        hidden_grad = hidden_grad.at[donor_pos].add(donor_grad.astype(jnp.float32))
        hidden_grad = hidden_grad.at[accept_pos].add(accept_grad.astype(jnp.float32))
        preact_grad = (hidden_grad * gelu_slope(preact)).astype(jnp.bfloat16)
        grad_padded = jnp.pad(preact_grad, ((reach_rows, reach_rows), (0, 0)))
        normed_grad = jnp.zeros((SEQ_LEN, CHANNELS), jnp.float32)
        for tap_index in range(TAPS):
            first_row = 2 * reach_rows - tap_index * DILATION
            normed_grad = normed_grad + lax.dot_general(grad_padded[first_row:first_row + SEQ_LEN], conv_weight[tap_index * CHANNELS:(tap_index + 1) * CHANNELS], (((1,), (1,)), ((), ())), preferred_element_type=jnp.float32)
        input_grad = norm_inverse * normed_grad - input_values * norm_inverse ** 3 * lax.optimization_barrier(jnp.mean(normed_grad * input_values, axis=1, keepdims=True))
        grads_out.append(input_grad.astype(jnp.bfloat16))
        conv_parts = [contract_rows(padded[tap_index * DILATION:tap_index * DILATION + SEQ_LEN], preact_grad) for tap_index in range(TAPS)]
        conv_total = conv_total + jnp.concatenate(conv_parts, axis=0)
        head_total = head_total + contract_rows(pair_feature, head_delta)
    weight_grads = jnp.concatenate([conv_total * (1.0 / math.sqrt(BATCH * SEQ_LEN)), head_total * (1.0 / math.sqrt(BATCH * PAIRS))], axis=0)
    return (jnp.stack(grads_out), weight_grads)
```

```python
import math

import jax
import jax.numpy as jnp
from jax import lax
from jax.sharding import PartitionSpec as P

DILATION = 8


def with_halo(cells, sides, width):
    for axis, dim in sides:
        count = lax.axis_size(axis)
        ends = count - 1
        head = lax.slice_in_dim(cells, 0, width, axis=dim)
        tail = lax.slice_in_dim(cells, cells.shape[dim] - width, cells.shape[dim], axis=dim)
        cells = jnp.concatenate(
            [
                lax.ppermute(tail, axis, [(i, (i + 1) % count) for i in range(ends)]),
                cells,
                lax.ppermute(head, axis, [((i + 1) % count, i) for i in range(ends)]),
            ],
            axis=dim,
        )
    return cells


def gelu_slope(values):
    normal_cdf = 0.5 * (1.0 + lax.erf(values * (1.0 / math.sqrt(2.0))))
    density = jnp.exp(-0.5 * values * values) * (1.0 / math.sqrt(2.0 * math.pi))
    return normal_cdf + values * density


def contract_rows(left_side, right_side):
    return lax.dot_general(
        left_side, right_side, (((0,), (0,)), ((), ())), preferred_element_type=jnp.float32
    )


def widened(field, reach_rows):
    return with_halo(field, (("seq", 0),), reach_rows)


def per_device(
    activations,
    conv_weight,
    head_first,
    head_second,
    hidden_cotangent,
    score_cotangent,
    donor_row,
    acceptor_owner,
    acceptor_row,
):
    row_count = activations.shape[1]
    chan_count = activations.shape[2]
    out_count = conv_weight.shape[1]
    tap_count = conv_weight.shape[0] // chan_count
    reach_rows = (tap_count - 1) // 2 * DILATION
    shards = lax.axis_size("seq")
    batch_total = lax.axis_size("dp") * activations.shape[0]
    pair_count = donor_row.shape[1]
    capacity = max(2, 2 * pair_count // shards)
    input_values = activations[0].astype(jnp.float32)
    norm_inverse = lax.rsqrt(jnp.mean(input_values * input_values, axis=1, keepdims=True) + 1e-05)
    normed = (input_values * norm_inverse).astype(jnp.bfloat16)
    padded = widened(normed, reach_rows)
    columns = jnp.concatenate(
        [
            padded[tap_index * DILATION : tap_index * DILATION + row_count]
            for tap_index in range(tap_count)
        ],
        axis=1,
    )
    preact = jnp.dot(columns, conv_weight, preferred_element_type=jnp.float32)
    hidden = jax.nn.gelu(preact, approximate=False).astype(jnp.bfloat16)
    owner_index = acceptor_owner[0, :, 0]
    owner_hits = (owner_index[:, None] == jnp.arange(shards, dtype=jnp.int32)[None, :]).astype(
        jnp.int32
    )
    earlier = jnp.cumsum(owner_hits, axis=0) - owner_hits
    slot_index = jnp.sum(earlier * owner_hits, axis=1)
    target = owner_index * capacity + slot_index
    request = (
        jnp.full((shards * capacity,), -1, jnp.int32)
        .at[target]
        .set(acceptor_row[0])
        .reshape(shards, capacity)
    )
    asked_rows = lax.all_to_all(request, "seq", split_axis=0, concat_axis=0, tiled=True)
    picked = jnp.take(hidden, jnp.maximum(asked_rows, 0), axis=0)
    returned = lax.all_to_all(picked, "seq", split_axis=0, concat_axis=0, tiled=True)
    accept_feat = returned.reshape(shards * capacity, out_count)[target]
    donor_feat = hidden[donor_row[0]]
    accept_values = accept_feat.astype(jnp.float32)
    donor_values = donor_feat.astype(jnp.float32)
    pair_feature = (donor_values * accept_values).astype(jnp.bfloat16)
    head_preact = jnp.dot(pair_feature, head_first, preferred_element_type=jnp.float32)
    head_delta = (
        score_cotangent[0][:, None]
        * head_second.astype(jnp.float32)[None, :]
        * gelu_slope(head_preact)
    ).astype(jnp.bfloat16)
    feature_grad = lax.dot_general(
        head_delta, head_first, (((1,), (1,)), ((), ())), preferred_element_type=jnp.float32
    )
    donor_grad = (feature_grad * accept_values).astype(jnp.bfloat16)
    accept_grad = (feature_grad * donor_values).astype(jnp.bfloat16)
    outgoing = (
        jnp.zeros((shards * capacity, out_count), jnp.bfloat16)
        .at[target]
        .set(accept_grad)
        .reshape(shards, capacity, out_count)
    )
    incoming = lax.all_to_all(outgoing, "seq", split_axis=0, concat_axis=0, tiled=True)
    row_ids = jnp.arange(row_count, dtype=jnp.int32)
    accept_hits = (asked_rows.reshape(-1)[:, None] == row_ids[None, :]).astype(jnp.bfloat16)
    donor_hits = (donor_row[0][:, None] == row_ids[None, :]).astype(jnp.bfloat16)
    hidden_grad = hidden_cotangent[0].astype(jnp.float32) + contract_rows(donor_hits, donor_grad)
    hidden_grad = hidden_grad + contract_rows(
        accept_hits, incoming.reshape(shards * capacity, out_count)
    )
    preact_grad = (hidden_grad * gelu_slope(preact)).astype(jnp.bfloat16)
    grad_padded = widened(preact_grad, reach_rows)
    spread = lax.dot_general(
        grad_padded, conv_weight, (((1,), (1,)), ((), ())), preferred_element_type=jnp.float32
    )
    normed_grad = spread[2 * reach_rows : 2 * reach_rows + row_count, 0:chan_count]
    for tap_index in range(1, tap_count):
        first_row = 2 * reach_rows - tap_index * DILATION
        normed_grad = (
            normed_grad
            + spread[
                first_row : first_row + row_count,
                tap_index * chan_count : (tap_index + 1) * chan_count,
            ]
        )
    input_grad = norm_inverse * normed_grad - input_values * norm_inverse**3 * jnp.mean(
        normed_grad * input_values, axis=1, keepdims=True
    )
    tap_rows = tap_count * chan_count
    chunk = (tap_rows + out_count) // shards
    sources = jnp.concatenate([columns, pair_feature], axis=1)
    sources = lax.all_to_all(sources, "seq", split_axis=1, concat_axis=0, tiled=True)
    sources = lax.all_gather(sources, "dp", axis=0, tiled=True)
    head_side = lax.all_to_all(head_delta, "dp", split_axis=1, concat_axis=0, tiled=True)
    head_side = lax.all_gather(
        head_side.reshape(-1, row_count, head_side.shape[1]), "seq", axis=1, tiled=True
    )
    conv_side = lax.all_to_all(preact_grad, "dp", split_axis=1, concat_axis=0, tiled=True)
    conv_side = lax.all_gather(
        conv_side.reshape(-1, row_count, conv_side.shape[1]), "seq", axis=1, tiled=True
    )
    conv_term = contract_rows(sources, conv_side.reshape(-1, conv_side.shape[2])) * (
        1.0 / math.sqrt(batch_total * row_count * shards)
    )
    head_term = contract_rows(sources, head_side.reshape(-1, head_side.shape[2])) * (
        1.0 / math.sqrt(batch_total * pair_count * shards)
    )
    row_of = lax.axis_index("seq") * chunk + jnp.arange(chunk, dtype=jnp.int32)
    weight_grads = jnp.where((row_of < tap_rows)[:, None], conv_term, head_term)
    return (input_grad.astype(jnp.bfloat16)[None], weight_grads)


def solution(mesh):
    placed = (
        P("dp", "seq", None),
        P(),
        P(),
        P(),
        P("dp", "seq", None),
        P("dp", "seq"),
        P("dp", "seq"),
        P("dp", "seq", None),
        P("dp", "seq"),
    )
    return jax.shard_map(
        per_device,
        mesh=mesh,
        in_specs=placed,
        out_specs=(P("dp", "seq", None), P("seq", "dp")),
        check_vma=False,
    )
```

```python
import math

import jax
import jax.numpy as jnp
from jax import lax
from jax.sharding import PartitionSpec as P

DILATION = 8


def with_halo(cells, sides, width):
    for axis, dim in sides:
        count = lax.axis_size(axis)
        ends = count - 1
        head = lax.slice_in_dim(cells, 0, width, axis=dim)
        tail = lax.slice_in_dim(cells, cells.shape[dim] - width, cells.shape[dim], axis=dim)
        cells = jnp.concatenate(
            [
                lax.ppermute(tail, axis, [(i, (i + 1) % count) for i in range(ends)]),
                cells,
                lax.ppermute(head, axis, [((i + 1) % count, i) for i in range(ends)]),
            ],
            axis=dim,
        )
    return cells


def gelu_slope(values):
    normal_cdf = 0.5 * (1.0 + lax.erf(values * (1.0 / math.sqrt(2.0))))
    density = jnp.exp(-0.5 * values * values) * (1.0 / math.sqrt(2.0 * math.pi))
    return normal_cdf + values * density


def contract_rows(left_side, right_side):
    return lax.dot_general(
        left_side, right_side, (((0,), (0,)), ((), ())), preferred_element_type=jnp.float32
    )


def widened(field, reach_rows):
    return with_halo(field, (("seq", 0),), reach_rows)


def per_device(
    activations,
    conv_weight,
    head_first,
    head_second,
    hidden_cotangent,
    score_cotangent,
    donor_row,
    acceptor_owner,
    acceptor_row,
):
    row_count = activations.shape[1]
    chan_count = activations.shape[2]
    out_count = conv_weight.shape[1]
    tap_count = conv_weight.shape[0] // chan_count
    reach_rows = (tap_count - 1) // 2 * DILATION
    shards = lax.axis_size("seq")
    batch_total = lax.axis_size("dp") * activations.shape[0]
    pair_count = donor_row.shape[1]
    capacity = max(2, 2 * pair_count // shards)
    input_values = activations[0].astype(jnp.float32)
    norm_inverse = lax.rsqrt(jnp.mean(input_values * input_values, axis=1, keepdims=True) + 1e-05)
    normed = (input_values * norm_inverse).astype(jnp.bfloat16)
    normed_all = lax.all_gather(normed, "seq", axis=0, tiled=True)
    padded = widened(normed, reach_rows)
    tap_rows = tap_count * chan_count
    columns = jnp.concatenate(
        [
            padded[tap_index * DILATION : tap_index * DILATION + row_count]
            for tap_index in range(tap_count)
        ],
        axis=1,
    )
    preact = jnp.dot(columns, conv_weight, preferred_element_type=jnp.float32)
    hidden = jax.nn.gelu(preact, approximate=False).astype(jnp.bfloat16)
    owner_index = acceptor_owner[0, :, 0]
    owner_hits = (owner_index[:, None] == jnp.arange(shards, dtype=jnp.int32)[None, :]).astype(
        jnp.int32
    )
    earlier = jnp.cumsum(owner_hits, axis=0) - owner_hits
    slot_index = jnp.sum(earlier * owner_hits, axis=1)
    target = owner_index * capacity + slot_index
    request = (
        jnp.full((shards * capacity,), -1, jnp.int32)
        .at[target]
        .set(acceptor_row[0])
        .reshape(shards, capacity)
    )
    asked_rows = lax.all_to_all(request, "seq", split_axis=0, concat_axis=0, tiled=True)
    picked = jnp.take(hidden, jnp.maximum(asked_rows, 0), axis=0)
    returned = lax.all_to_all(picked, "seq", split_axis=0, concat_axis=0, tiled=True)
    accept_feat = returned.reshape(shards * capacity, out_count)[target]
    donor_feat = hidden[donor_row[0]]
    accept_values = accept_feat.astype(jnp.float32)
    donor_values = donor_feat.astype(jnp.float32)
    pair_feature = (donor_values * accept_values).astype(jnp.bfloat16)
    head_preact = jnp.dot(pair_feature, head_first, preferred_element_type=jnp.float32)
    head_delta = (
        score_cotangent[0][:, None]
        * head_second.astype(jnp.float32)[None, :]
        * gelu_slope(head_preact)
    ).astype(jnp.bfloat16)
    feature_grad = lax.dot_general(
        head_delta, head_first, (((1,), (1,)), ((), ())), preferred_element_type=jnp.float32
    )
    donor_grad = (feature_grad * accept_values).astype(jnp.bfloat16)
    accept_grad = (feature_grad * donor_values).astype(jnp.bfloat16)
    outgoing = (
        jnp.zeros((shards * capacity, out_count), jnp.bfloat16)
        .at[target]
        .set(accept_grad)
        .reshape(shards, capacity, out_count)
    )
    incoming = lax.all_to_all(outgoing, "seq", split_axis=0, concat_axis=0, tiled=True)
    row_ids = jnp.arange(row_count, dtype=jnp.int32)
    accept_hits = (asked_rows.reshape(-1)[:, None] == row_ids[None, :]).astype(jnp.bfloat16)
    donor_hits = (donor_row[0][:, None] == row_ids[None, :]).astype(jnp.bfloat16)
    hidden_grad = hidden_cotangent[0].astype(jnp.float32) + contract_rows(donor_hits, donor_grad)
    hidden_grad = hidden_grad + contract_rows(
        accept_hits, incoming.reshape(shards * capacity, out_count)
    )
    preact_grad = (hidden_grad * gelu_slope(preact)).astype(jnp.bfloat16)
    grad_padded = widened(preact_grad, reach_rows)
    spread = lax.dot_general(
        grad_padded, conv_weight, (((1,), (1,)), ((), ())), preferred_element_type=jnp.float32
    )
    normed_grad = spread[2 * reach_rows : 2 * reach_rows + row_count, 0:chan_count]
    for tap_index in range(1, tap_count):
        first_row = 2 * reach_rows - tap_index * DILATION
        normed_grad = (
            normed_grad
            + spread[
                first_row : first_row + row_count,
                tap_index * chan_count : (tap_index + 1) * chan_count,
            ]
        )
    input_grad = norm_inverse * normed_grad - input_values * norm_inverse**3 * jnp.mean(
        normed_grad * input_values, axis=1, keepdims=True
    )
    chunk = (tap_rows + out_count) // shards
    first = lax.axis_index("seq") * chunk
    tap_low = jnp.minimum(first // chan_count, tap_count - 1)
    tap_high = jnp.minimum(tap_low + 1, tap_count - 1)
    all_rows = row_count * shards
    gathered = jnp.pad(normed_all, ((reach_rows, reach_rows), (0, 0)))
    pair_of_taps = jnp.concatenate(
        [
            lax.dynamic_slice_in_dim(gathered, tap_low * DILATION, all_rows, axis=0),
            lax.dynamic_slice_in_dim(gathered, tap_high * DILATION, all_rows, axis=0),
        ],
        axis=1,
    )
    sources = lax.dynamic_slice_in_dim(pair_of_taps, first % chan_count, chunk, axis=1)
    grad_all = lax.all_gather(preact_grad, "seq", axis=0, tiled=True)
    conv_term = contract_rows(sources, grad_all) * (
        1.0 / math.sqrt(batch_total * row_count * shards)
    )
    parts = lax.all_to_all(
        conv_term.astype(jnp.bfloat16), "dp", split_axis=1, concat_axis=0, tiled=True
    ).reshape(-1, chunk, out_count // lax.axis_size("dp"))
    conv_share = jnp.sum(parts.astype(jnp.float32), axis=0)
    head_term = contract_rows(pair_feature, head_delta) * (
        1.0 / math.sqrt(batch_total * pair_count * shards)
    )
    head_cells = lax.all_to_all(
        head_term.astype(jnp.bfloat16), "dp", split_axis=1, concat_axis=0, tiled=True
    ).reshape(-1, out_count, out_count // lax.axis_size("dp"))
    head_share = jnp.sum(head_cells.astype(jnp.float32), axis=0)
    head_parts = lax.all_to_all(
        head_share.astype(jnp.bfloat16), "seq", split_axis=0, concat_axis=0, tiled=True
    )
    block = out_count // shards
    head_block = jnp.sum(
        head_parts.reshape(shards, block, -1).astype(jnp.float32), axis=0
    )
    per_owner = tap_count * chan_count // out_count + 1
    skipped = tap_rows // block
    head_rows = jnp.concatenate(
        [
            lax.ppermute(
                head_block,
                "seq",
                [
                    (i, (skipped + i) // per_owner)
                    for i in range(shards)
                    if (skipped + i) % per_owner == place
                ],
            )
            for place in range(per_owner)
        ],
        axis=0,
    )
    row_of = first + jnp.arange(chunk, dtype=jnp.int32)
    weight_grads = jnp.where((row_of < tap_rows)[:, None], conv_share, head_rows)
    return (input_grad.astype(jnp.bfloat16)[None], weight_grads)


def solution(mesh):
    placed = (
        P("dp", "seq", None),
        P(),
        P(),
        P(),
        P("dp", "seq", None),
        P("dp", "seq"),
        P("dp", "seq"),
        P("dp", "seq", None),
        P("dp", "seq"),
    )
    return jax.shard_map(
        per_device,
        mesh=mesh,
        in_specs=placed,
        out_specs=(P("dp", "seq", None), P("seq", "dp")),
        check_vma=False,
    )
```

```python
import math

import jax
import jax.numpy as jnp
from jax import lax
from jax.sharding import PartitionSpec as P

DILATION = 8


def with_halo(cells, sides, width):
    for axis, dim in sides:
        count = lax.axis_size(axis)
        ends = count - 1
        head = lax.slice_in_dim(cells, 0, width, axis=dim)
        tail = lax.slice_in_dim(cells, cells.shape[dim] - width, cells.shape[dim], axis=dim)
        cells = jnp.concatenate(
            [
                lax.ppermute(tail, axis, [(i, (i + 1) % count) for i in range(ends)]),
                cells,
                lax.ppermute(head, axis, [((i + 1) % count, i) for i in range(ends)]),
            ],
            axis=dim,
        )
    return cells


def gelu_slope(values):
    normal_cdf = 0.5 * (1.0 + lax.erf(values * (1.0 / math.sqrt(2.0))))
    density = jnp.exp(-0.5 * values * values) * (1.0 / math.sqrt(2.0 * math.pi))
    return normal_cdf + values * density


def contract_rows(left_side, right_side):
    return lax.dot_general(
        left_side, right_side, (((0,), (0,)), ((), ())), preferred_element_type=jnp.float32
    )


def widened(field, reach_rows):
    return with_halo(field, (("seq", 0),), reach_rows)


def scaled(rows):
    values = rows.astype(jnp.float32)
    inverse = lax.rsqrt(jnp.mean(values * values, axis=1, keepdims=True) + 1e-05)
    return (values * inverse).astype(jnp.bfloat16)


def per_device(
    activations,
    conv_weight,
    head_first,
    head_second,
    hidden_cotangent,
    score_cotangent,
    donor_row,
    acceptor_owner,
    acceptor_row,
):
    row_count = activations.shape[1]
    chan_count = activations.shape[2]
    out_count = conv_weight.shape[1]
    tap_count = conv_weight.shape[0] // chan_count
    reach_rows = (tap_count - 1) // 2 * DILATION
    shards = lax.axis_size("seq")
    batch_total = lax.axis_size("dp") * activations.shape[0]
    pair_count = donor_row.shape[1]
    capacity = max(2, 2 * pair_count // shards)
    input_values = activations[0].astype(jnp.float32)
    norm_inverse = lax.rsqrt(jnp.mean(input_values * input_values, axis=1, keepdims=True) + 1e-05)
    normed_all = scaled(lax.all_gather(activations[0], "seq", axis=0, tiled=True))
    padded = scaled(widened(activations[0], reach_rows))
    tap_rows = tap_count * chan_count
    columns = jnp.concatenate(
        [
            padded[tap_index * DILATION : tap_index * DILATION + row_count]
            for tap_index in range(tap_count)
        ],
        axis=1,
    )
    preact = jnp.dot(columns, conv_weight, preferred_element_type=jnp.float32)
    hidden = jax.nn.gelu(preact, approximate=False).astype(jnp.bfloat16)
    owner_index = acceptor_owner[0, :, 0]
    owner_hits = (owner_index[:, None] == jnp.arange(shards, dtype=jnp.int32)[None, :]).astype(
        jnp.int32
    )
    earlier = jnp.cumsum(owner_hits, axis=0) - owner_hits
    slot_index = jnp.sum(earlier * owner_hits, axis=1)
    target = owner_index * capacity + slot_index
    request = (
        jnp.full((shards * capacity,), -1, jnp.int32)
        .at[target]
        .set(acceptor_row[0])
        .reshape(shards, capacity)
    )
    asked_rows = lax.all_to_all(request, "seq", split_axis=0, concat_axis=0, tiled=True)
    picked = jnp.take(hidden, jnp.maximum(asked_rows, 0), axis=0)
    returned = lax.all_to_all(picked, "seq", split_axis=0, concat_axis=0, tiled=True)
    accept_feat = returned.reshape(shards * capacity, out_count)[target]
    donor_feat = hidden[donor_row[0]]
    accept_values = accept_feat.astype(jnp.float32)
    donor_values = donor_feat.astype(jnp.float32)
    pair_feature = (donor_values * accept_values).astype(jnp.bfloat16)
    head_preact = jnp.dot(pair_feature, head_first, preferred_element_type=jnp.float32)
    head_delta = (
        score_cotangent[0][:, None]
        * head_second.astype(jnp.float32)[None, :]
        * gelu_slope(head_preact)
    ).astype(jnp.bfloat16)
    feature_grad = lax.dot_general(
        head_delta, head_first, (((1,), (1,)), ((), ())), preferred_element_type=jnp.float32
    )
    donor_grad = (feature_grad * accept_values).astype(jnp.bfloat16)
    accept_grad = (feature_grad * donor_values).astype(jnp.bfloat16)
    outgoing = (
        jnp.zeros((shards * capacity, out_count), jnp.bfloat16)
        .at[target]
        .set(accept_grad)
        .reshape(shards, capacity, out_count)
    )
    incoming = lax.all_to_all(outgoing, "seq", split_axis=0, concat_axis=0, tiled=True)
    row_ids = jnp.arange(row_count, dtype=jnp.int32)
    accept_hits = (asked_rows.reshape(-1)[:, None] == row_ids[None, :]).astype(jnp.bfloat16)
    donor_hits = (donor_row[0][:, None] == row_ids[None, :]).astype(jnp.bfloat16)
    hidden_grad = hidden_cotangent[0].astype(jnp.float32) + contract_rows(donor_hits, donor_grad)
    hidden_grad = hidden_grad + contract_rows(
        accept_hits, incoming.reshape(shards * capacity, out_count)
    )
    preact_grad = (hidden_grad * gelu_slope(preact)).astype(jnp.bfloat16)
    grad_padded = widened(preact_grad, reach_rows)
    spread = lax.dot_general(
        grad_padded, conv_weight, (((1,), (1,)), ((), ())), preferred_element_type=jnp.float32
    )
    normed_grad = spread[2 * reach_rows : 2 * reach_rows + row_count, 0:chan_count]
    for tap_index in range(1, tap_count):
        first_row = 2 * reach_rows - tap_index * DILATION
        normed_grad = (
            normed_grad
            + spread[
                first_row : first_row + row_count,
                tap_index * chan_count : (tap_index + 1) * chan_count,
            ]
        )
    input_grad = norm_inverse * normed_grad - input_values * norm_inverse**3 * jnp.mean(
        normed_grad * input_values, axis=1, keepdims=True
    )
    chunk = (tap_rows + out_count) // shards
    first = lax.axis_index("seq") * chunk
    tap_low = jnp.minimum(first // chan_count, tap_count - 1)
    tap_high = jnp.minimum(tap_low + 1, tap_count - 1)
    all_rows = row_count * shards
    gathered = jnp.pad(normed_all, ((reach_rows, reach_rows), (0, 0)))
    pair_of_taps = jnp.concatenate(
        [
            lax.dynamic_slice_in_dim(gathered, tap_low * DILATION, all_rows, axis=0),
            lax.dynamic_slice_in_dim(gathered, tap_high * DILATION, all_rows, axis=0),
        ],
        axis=1,
    )
    sources = lax.dynamic_slice_in_dim(pair_of_taps, first % chan_count, chunk, axis=1)
    grad_all = lax.all_gather(preact_grad, "seq", axis=0, tiled=True)
    conv_term = contract_rows(sources, grad_all) * (
        1.0 / math.sqrt(batch_total * row_count * shards)
    )
    parts = lax.all_to_all(
        conv_term.astype(jnp.bfloat16), "dp", split_axis=1, concat_axis=0, tiled=True
    ).reshape(-1, chunk, out_count // lax.axis_size("dp"))
    conv_share = jnp.sum(parts.astype(jnp.float32), axis=0)
    head_term = contract_rows(pair_feature, head_delta) * (
        1.0 / math.sqrt(batch_total * pair_count * shards)
    )
    head_cells = lax.all_to_all(
        head_term.astype(jnp.bfloat16), "dp", split_axis=1, concat_axis=0, tiled=True
    ).reshape(-1, out_count, out_count // lax.axis_size("dp"))
    head_share = jnp.sum(head_cells.astype(jnp.float32), axis=0)
    head_parts = lax.all_to_all(
        head_share.astype(jnp.bfloat16), "seq", split_axis=0, concat_axis=0, tiled=True
    )
    block = out_count // shards
    head_block = jnp.sum(
        head_parts.reshape(shards, block, -1).astype(jnp.float32), axis=0
    )
    per_owner = tap_count * chan_count // out_count + 1
    skipped = tap_rows // block
    head_rows = jnp.concatenate(
        [
            lax.ppermute(
                head_block,
                "seq",
                [
                    (i, (skipped + i) // per_owner)
                    for i in range(shards)
                    if (skipped + i) % per_owner == place
                ],
            )
            for place in range(per_owner)
        ],
        axis=0,
    )
    row_of = first + jnp.arange(chunk, dtype=jnp.int32)
    weight_grads = jnp.where((row_of < tap_rows)[:, None], conv_share, head_rows)
    return (input_grad.astype(jnp.bfloat16)[None], weight_grads)


def solution(mesh):
    placed = (
        P("dp", "seq", None),
        P(),
        P(),
        P(),
        P("dp", "seq", None),
        P("dp", "seq"),
        P("dp", "seq"),
        P("dp", "seq", None),
        P("dp", "seq"),
    )
    return jax.shard_map(
        per_device,
        mesh=mesh,
        in_specs=placed,
        out_specs=(P("dp", "seq", None), P("seq", "dp")),
        check_vma=False,
    )
```
